32 devices in a mesh: groups: 2 (over y), blk: 4 (over z), dp: 2 (over x), sub: 2 (over core).
Axes of the slice: x: 2, y: 2, z: 4, core: 2. Of those that a mesh axis runs over, the one named last changes fastest.
Arguments:
- cls_feats: bfloat16 [4096, 1024], P(('groups', 'blk', 'dp', 'sub')), parts along dimension 0, may hold values from -6 to 6
- proj: bfloat16 [1024, 768], replicated, may hold values from -0.1875 to 0.1875
- cluster_id: int32 [4096, 1], P(('groups', 'blk', 'dp', 'sub')), parts along dimension 0, may hold values from 0 to 7; in each aligned block of 128 rows (0 to 127, 128 to 255, ...) at most 32 rows name the same one
- row_index: int32 [4096], P(('groups', 'blk', 'dp', 'sub')), parts along dimension 0, may hold values from 0 to 2047, each once
- assign: int32 [16], P('groups'), parts along dimension 0, may hold values from 0 to 7, each once
Outputs:
- best_cos: float32 [4096], P(('groups', 'blk', 'dp', 'sub')), parts along dimension 0
The draws below stay inside these ranges and needn't reach their ends.
There are 2 independent parts, one for each index of `groups`. The reference program is written for one: setup_inputs(seed, part) draws one part's arguments, and reference() takes and returns one part's arrays. A program takes and returns all parts, laid end to end along the dimension named above; an argument that names none is the same for every part. Nothing has to cross between parts.
Inputs may be any that keep to these rules, and one draw needn't show every extreme that they name: `cluster_id`: among the 128 images of one device, at most 32 lie in one fine cluster; some device has exactly 32 in some fine cluster, and every fine cluster has some image. `row_index`: every number appears once. `assign`: every number appears once.
All inputs are finite; a program needn't handle non-finite values.
Results may differ from the reference program's by a relative error of at most 0.0015.
Values may be sent and summed in bfloat16 or wider, within the bound.
A program may use at most 64 MiB of HBM per device.

```python
import math
import jax
import jax.numpy as jnp
import numpy as np
from jax import lax

D = 1024
E = 768
IMG_DEV = 128
SUBCL = 4
K_FINE = 8
MOSTF = 32
IMAGES = 2048
N_BLK = 4
N_DP = 2
N_SUB = 2


def levels(rng, dims, cuts, smallest, high):
    loudness, own = 1.0, jax.random.fold_in(rng, 6)
    for dim, shards_of in cuts:
        draws = jnp.exp(jax.random.uniform(jax.random.fold_in(own, dim), (shards_of,), jnp.float32, smallest / len(cuts), high / len(cuts)))
        loudness = loudness * jnp.repeat(draws, dims[dim] // shards_of).reshape([-1 if axis == dim else 1 for axis in range(len(dims))])
    return loudness


def shared_out(key, own, number, rows, amount, top, most, skew):
    sequence = jax.random.permutation(key, amount)
    heavy_load, ordinary = portions_of(amount, rows * top, most, skew, True), portions_of(amount, rows * top, most, skew, False)
    places = jnp.arange(amount)

    def named(lengths, rotation):
        used = int((lengths > 0).sum())
        fixed = max(1, used // 4)
        shifted = fixed + (places - fixed + rotation * (used - fixed)) % max(1, amount - fixed)
        return jnp.zeros((amount,), jnp.int32).at[sequence[jnp.where(places < fixed, places, shifted)]].set(jnp.asarray(lengths, jnp.int32))

    lengths = jnp.where(number % 4 == 0, named(heavy_load, number // 4), named(ordinary, number - number // 4 - 1))
    mixed = jax.random.permutation(jax.random.fold_in(own, 3), amount)
    giver, receiver = mixed[0:amount // 2 * 2:2], mixed[1:amount // 2 * 2:2]
    room = jnp.minimum(lengths[giver] - 1, most - lengths[receiver]) // 2
    room = jnp.where((giver == sequence[0]) | (receiver == sequence[0]) | (lengths[receiver] == 0), 0, jnp.maximum(room, 0))
    shifted = jax.random.randint(jax.random.fold_in(own, 4), (amount // 2,), 0, 1 << 20) % (room + 1)
    lengths = lengths.at[giver].add(-shifted).at[receiver].add(shifted)
    members = jnp.searchsorted(jnp.cumsum(lengths), jnp.arange(rows * top), side="right").astype(jnp.int32)
    listing = members.reshape(top, rows).T
    listing = listing[jax.random.permutation(jax.random.fold_in(own, 1), rows)]
    rotation = jax.random.randint(jax.random.fold_in(own, 2), (rows, 1), 0, top)
    return jnp.take_along_axis(listing, (jnp.arange(top)[None, :] + rotation) % top, axis=1)


def portions_of(number_of, total, reach, skew, full):
    weights = [(1 << 20) // math.isqrt(rank ** skew) + 1 for rank in range(1, number_of + 1)]
    largest = reach if full else min(reach, max(-(-total // number_of), total * weights[0] // sum(weights)))
    least = 1 if total - largest >= number_of - 1 else 0
    given, rest = [largest] + [least] * (number_of - 1), total - largest - least * (number_of - 1)
    while rest > 0:
        free = [i for i in range(1, number_of) if given[i] < largest] or [i for i in range(1, number_of) if given[i] < reach]
        pool, left = sum([weights[i] for i in free]), rest
        for i in free:
            addition = min(reach - given[i], max(1, left * weights[i] // pool), rest)
            given[i] = given[i] + addition
            rest = rest - addition
    return np.array(given)


def gaussian(rng, dims, width, bound, shards=(), kind=jnp.bfloat16):
    gain = levels(rng, dims, shards, -0.22, 0.18) if shards else 1.0
    values = jax.random.normal(rng, dims, jnp.float32) * width * gain
    return jnp.minimum(jnp.maximum(values, -bound), bound).astype(kind)


def setup_inputs(seed: int = 0, part: int = 0) -> dict:
    arg_keys = jax.random.split(jax.random.key(seed), 6)
    part_keys = jax.random.split(jax.random.fold_in(arg_keys[5], part), 6)
    cls_feats = gaussian(part_keys[0], (IMAGES, D), 1.0, 6.0, ((0, 16),))
    proj = gaussian(arg_keys[1], (D, E), D ** -0.5, 0.1875)
    cluster_id_keys = jax.random.split(jax.random.fold_in(part_keys[2], 1), IMAGES // IMG_DEV)
    cluster_id_turns = jax.random.permutation(jax.random.fold_in(part_keys[2], 3), IMAGES // IMG_DEV)
    cluster_id = jax.vmap(lambda own, number: shared_out(jax.random.fold_in(part_keys[2], 2), own, number, IMG_DEV, K_FINE, 1, MOSTF, 2))(cluster_id_keys, cluster_id_turns).reshape((IMAGES, 1))
    row_index = jax.random.permutation(part_keys[3], IMAGES).astype(jnp.int32)
    assign = jax.random.permutation(part_keys[4], K_FINE).astype(jnp.int32)
    return {"cls_feats": cls_feats, "proj": proj, "cluster_id": cluster_id, "row_index": row_index, "assign": assign}


empty_mark = 2 ** 30

def embed(cls_feats, proj):
    feats = cls_feats.astype(jnp.float32)
    center = lax.optimization_barrier(jnp.mean(feats, axis=1, keepdims=True))
    spread = lax.optimization_barrier(jnp.mean((feats - center) ** 2, axis=1, keepdims=True))
    normed = ((feats - center) * lax.rsqrt(spread + 1e-05)).astype(jnp.bfloat16)
    proj_out = jnp.dot(normed, proj, preferred_element_type=jnp.float32)
    scale = lax.rsqrt(lax.optimization_barrier(jnp.sum(proj_out * proj_out, axis=1, keepdims=True)) + 1e-06)
    return (proj_out * scale).astype(jnp.bfloat16)

def reference(cls_feats, proj, cluster_id, row_index, assign):
    emb = embed(cls_feats, proj)
    devices = N_BLK * N_DP * N_SUB
    capacity = devices * SUBCL * MOSTF
    fine = cluster_id[:, 0]
    onehot = (fine[:, None] == jnp.arange(K_FINE, dtype=jnp.int32)[None, :]).astype(jnp.int32)
    per_device = onehot.reshape(devices, IMG_DEV, K_FINE)
    earlier = (jnp.cumsum(per_device, axis=1) - per_device).reshape(IMAGES, K_FINE)
    rank = lax.optimization_barrier(jnp.sum(earlier * onehot, axis=1)).astype(jnp.int32)
    place = assign[fine]
    coarse = (place // SUBCL).astype(jnp.int32)
    device_of = (jnp.arange(IMAGES, dtype=jnp.int32) // IMG_DEV).astype(jnp.int32)
    position = (device_of * (SUBCL * MOSTF) + place % SUBCL * MOSTF + rank).astype(jnp.int32)
    table_emb = jnp.zeros((N_DP, capacity, E), emb.dtype).at[coarse, position].set(emb)
    table_idx = jnp.full((N_DP, capacity), empty_mark, jnp.int32).at[coarse, position].set(row_index)
    block = math.gcd(capacity, 512)

    def per_group(pair):
        group_emb, group_idx = pair

        def per_block(rows):
            row_emb, row_idx = rows
            scores = jnp.dot(row_emb, group_emb.T, preferred_element_type=jnp.float32)
            scores = jnp.where(group_idx[None, :] < row_idx[:, None], scores, -1.0)
            return jnp.maximum(lax.optimization_barrier(jnp.max(scores, axis=1)), -1.0)
        parts = (group_emb.reshape(capacity // block, block, E), group_idx.reshape(capacity // block, block))
        return lax.map(per_block, parts).reshape(capacity)
    result = lax.map(per_group, (table_emb, table_idx))
    return result[coarse, position]
```

```python
import functools

import jax
import jax.numpy as jnp
from jax import lax
from jax.experimental import pallas as pl
from jax.experimental.pallas import tpu as pltpu
from jax.sharding import PartitionSpec as P

MESH = pl.DeviceIdType.MESH
NT = (((1,), (1,)), ((), ()))


def each(start, stop, body):
    if stop - start <= 4:
        for i in range(start, stop):
            body(i)
    else:
        lax.fori_loop(start, stop, lambda i, _: (body(i), None)[1], None)


def kernel(
    n_blk, n_dp, n_sub, images,
    feats_hbm, proj_hbm, cid_ref, idx_ref, assign_ref,
    out_ref,
    feats_ref, proj_ref, plane, plane_key, far, far_key, part_out, part_in, ret_out, ret_in,
    load_sem, pe_send, pe_recv, pk_send, pk_recv, fe_send, fe_recv, fk_send, fk_recv,
    po_send, po_recv, re_send, re_recv,
):
    n_plane = n_dp * n_sub
    n_far = n_blk // 2
    whole_far = (n_blk - 1) // 2
    z, x, c = lax.axis_index("blk"), lax.axis_index("dp"), lax.axis_index("sub")
    rows = idx_ref.shape[1]

    def in_plane(k, sign):
        dx, dc = lax.div(k, n_sub), lax.rem(k, n_sub)
        if sign < 0:
            dx, dc = n_dp - dx, n_sub - dc
        return {"blk": z, "dp": lax.rem(x + dx, n_dp), "sub": lax.rem(c + dc, n_sub)}

    def across(d, sign):
        return {"blk": lax.rem(z + (d if sign > 0 else n_blk - d), n_blk), "dp": x, "sub": c}

    half = n_blk // 2
    lower = z < half
    within = jnp.where(lower, z, z - half)
    sends_half = (lax.rem(within, 2) == 0) == lower
    has_half = n_far > whole_far

    load_feats = pltpu.make_async_copy(feats_hbm, feats_ref, load_sem.at[0])
    load_proj = pltpu.make_async_copy(proj_hbm, proj_ref, load_sem.at[1])
    load_feats.start()
    load_proj.start()

    barrier = pltpu.get_barrier_semaphore()

    def greet(device):
        pl.semaphore_signal(barrier, inc=1, device_id=device, device_id_type=MESH)

    each(1, n_plane, lambda k: greet(in_plane(k, 1)))

    def greet_far(d):
        greet(across(d, 1))
        greet(across(d, -1))

    each(1, whole_far + 1, greet_far)
    if has_half:
        greet(across(half, 1))
    pl.semaphore_wait(barrier, n_plane - 1 + 2 * whole_far + (1 if has_half else 0))

    def remote(src, dst, send, recv, device):
        return pltpu.make_async_remote_copy(
            src_ref=src, dst_ref=dst, send_sem=send, recv_sem=recv,
            device_id=device, device_id_type=MESH,
        )

    def plane_emb_copy(k):
        return remote(plane.at[0], plane.at[k], pe_send.at[k], pe_recv.at[k], in_plane(k, 1))

    def plane_key_copy(k):
        return remote(plane_key.at[0], plane_key.at[k], pk_send.at[k], pk_recv.at[k], in_plane(k, 1))

    def far_emb_copy(d):
        return remote(plane.at[0], far.at[d - 1], fe_send.at[d - 1], fe_recv.at[d - 1], across(d, 1))

    def far_key_copy(d):
        return remote(plane_key.at[0], far_key.at[d - 1], fk_send.at[d - 1], fk_recv.at[d - 1], across(d, 1))

    def part_copy(k):
        return remote(part_out.at[k], part_in.at[k], po_send.at[k], po_recv.at[k], in_plane(k, -1))

    def ret_copy(d):
        return remote(ret_out.at[d - 1], ret_in.at[d - 1], re_send.at[d - 1], re_recv.at[d - 1], across(d, -1))

    per_coarse = assign_ref.shape[0] // n_dp
    cid = cid_ref[...]
    base = jnp.zeros_like(cid)
    for f in range(assign_ref.shape[0]):
        base = jnp.where(cid == f, lax.div(assign_ref[f], per_coarse) * images, base)
    key = base + idx_ref[...]
    sub_row = lax.broadcasted_iota(jnp.int32, (8, rows), 0)
    plane_key[0] = jnp.where(
        sub_row == 0, jnp.broadcast_to(key, (8, rows)), jnp.broadcast_to(base, (8, rows))
    )
    each(1, whole_far + 1, lambda d: far_key_copy(d).start())
    if has_half:
        pl.when(sends_half)(lambda: far_key_copy(half).start())
    each(1, n_plane, lambda k: plane_key_copy(k).start())

    load_feats.wait()
    feats = feats_ref[...].astype(jnp.float32)
    center = jnp.mean(feats, axis=1, keepdims=True)
    shifted = feats - center
    spread = jnp.mean(shifted * shifted, axis=1, keepdims=True)
    normed = (shifted * lax.rsqrt(spread + 1e-05)).astype(jnp.bfloat16)
    load_proj.wait()
    proj_out = jnp.dot(normed, proj_ref[...], preferred_element_type=jnp.float32)
    scale = lax.rsqrt(jnp.sum(proj_out * proj_out, axis=1, keepdims=True) + 1e-06)
    plane[0] = (proj_out * scale).astype(jnp.bfloat16)

    if has_half:
        pl.when(sends_half)(lambda: far_emb_copy(half).start())
    each(1, whole_far + 1, lambda d: far_emb_copy(d).start())
    each(1, n_plane, lambda k: plane_emb_copy(n_plane - k).start())

    def column(key_row):
        return jnp.transpose(jnp.broadcast_to(key_row, (rows, rows)))

    def lane_best(scores):
        return jnp.max(jnp.transpose(scores), axis=0, keepdims=True)

    def spread8(row):
        return jnp.broadcast_to(row, (8, rows))

    own_col = column(plane_key[0][0:1])

    def own_step(k, best):
        keys = plane_key[k]
        k_row, b_row = keys[0:1], keys[1:2]
        scores = lax.dot_general(plane[0], plane[k], NT, preferred_element_type=jnp.float32)
        good = (own_col >= b_row) & (own_col < b_row + images) & (own_col > k_row)
        return jnp.maximum(best, jnp.where(good, scores, -1.0))

    def arrived(k):
        plane_key_copy(k).wait_recv()
        plane_emb_copy(k).wait_recv()

    best = own_step(0, jnp.full((rows, rows), -1.0, jnp.float32))
    if n_plane <= 4:
        for k in range(1, n_plane):
            arrived(k)
            best = own_step(k, best)
    else:
        best = lax.fori_loop(1, n_plane, lambda k, b: (arrived(k), own_step(k, b))[1], best)
    total = lane_best(best)

    def far_step(d, first):
        far_key_copy(d).wait_recv()
        far_emb_copy(d).wait_recv()
        col = column(far_key[d - 1][0:1])

        def step(k, best):
            keys = plane_key[k]
            k_row, b_row = keys[0:1], keys[1:2]
            scores = lax.dot_general(far[d - 1], plane[k], NT, preferred_element_type=jnp.float32)
            scores = jnp.where((col >= b_row) & (col < b_row + images), scores, -1.0)
            low = col < k_row
            gain = spread8(jnp.max(jnp.where(low, scores, -1.0), axis=0, keepdims=True))
            if first:
                part_out[k] = gain
            else:
                part_out[k] = jnp.maximum(part_out[k], gain)
            return jnp.maximum(best, jnp.where(low, -1.0, scores))

        best = jnp.full((rows, rows), -1.0, jnp.float32)
        if n_plane <= 4:
            for k in range(n_plane):
                best = step(k, best)
        else:
            best = lax.fori_loop(0, n_plane, step, best)
        ret_out[d - 1] = spread8(lane_best(best))
        ret_copy(d).start()

    if whole_far == 0:
        part_out[...] = jnp.full(part_out.shape, -1.0, jnp.float32)
    else:
        far_step(1, True)
        each(2, whole_far + 1, lambda d: far_step(d, False))
    if has_half:
        pl.when(jnp.logical_not(sends_half))(lambda: far_step(half, False))
    each(1, n_plane, lambda k: part_copy(k).start())

    total = jnp.maximum(total, part_out[0][0:1])

    def take_part(k, total):
        part_copy(k).wait_recv()
        return jnp.maximum(total, part_in[k][0:1])

    def take_ret(d, total):
        ret_copy(d).wait_recv()
        return jnp.maximum(total, ret_in[d - 1][0:1])

    out_ref[...] = jnp.full(out_ref.shape, -1.0, jnp.float32)
    for d in range(1, whole_far + 1):
        total = take_ret(d, total)
    for k in range(1, n_plane):
        total = take_part(k, total)
    out_ref[...] = total
    if has_half:

        @pl.when(sends_half)
        def _():
            out_ref[...] = take_ret(half, out_ref[...])

    def sent_far(d):
        far_key_copy(d).wait_send()
        far_emb_copy(d).wait_send()

    def sent_plane(k):
        plane_key_copy(k).wait_send()
        plane_emb_copy(k).wait_send()
        part_copy(k).wait_send()

    each(1, whole_far + 1, sent_far)
    each(1, whole_far + 1, lambda d: ret_copy(d).wait_send())
    if has_half:
        pl.when(sends_half)(lambda: sent_far(half))
        pl.when(jnp.logical_not(sends_half))(lambda: ret_copy(half).wait_send())
    each(1, n_plane, sent_plane)


def local(n_blk, n_dp, n_sub, cls_feats, proj, cluster_id, row_index, assign):
    rows, depth = cls_feats.shape
    width = proj.shape[1]
    n_plane, n_far = n_dp * n_sub, max(1, n_blk // 2)
    images = rows * n_blk * n_plane
    vmem, dma = pltpu.VMEM, pltpu.SemaphoreType.DMA
    out = pl.pallas_call(
        functools.partial(kernel, n_blk, n_dp, n_sub, images),
        out_shape=jax.ShapeDtypeStruct((1, rows), jnp.float32),
        in_specs=[
            pl.BlockSpec(memory_space=pl.ANY),
            pl.BlockSpec(memory_space=pl.ANY),
            pl.BlockSpec(memory_space=vmem),
            pl.BlockSpec(memory_space=vmem),
            pl.BlockSpec(memory_space=pltpu.SMEM),
        ],
        out_specs=pl.BlockSpec(memory_space=vmem),
        scratch_shapes=[
            vmem((rows, depth), cls_feats.dtype),
            vmem((depth, width), proj.dtype),
            vmem((n_plane, rows, width), jnp.bfloat16),
            vmem((n_plane, 8, rows), jnp.int32),
            vmem((n_far, rows, width), jnp.bfloat16),
            vmem((n_far, 8, rows), jnp.int32),
            vmem((n_plane, 8, rows), jnp.float32),
            vmem((n_plane, 8, rows), jnp.float32),
            vmem((n_far, 8, rows), jnp.float32),
            vmem((n_far, 8, rows), jnp.float32),
            dma((2,)),
            *[dma((n_plane,))] * 4,
            *[dma((n_far,))] * 4,
            *[dma((n_plane,))] * 2,
            *[dma((n_far,))] * 2,
        ],
        compiler_params=pltpu.CompilerParams(
            collective_id=0, has_side_effects=True, vmem_limit_bytes=32 * 2**20
        ),
    )(cls_feats, proj, cluster_id.reshape(1, rows), row_index.reshape(1, rows), assign)
    return out.reshape(rows)


def solution(mesh):
    split = ("groups", "blk", "dp", "sub")
    in_specs = (P(split, None), P(), P(split, None), P(split), P("groups"))
    body = functools.partial(local, mesh.shape["blk"], mesh.shape["dp"], mesh.shape["sub"])
    return jax.shard_map(body, mesh=mesh, in_specs=in_specs, out_specs=P(split), check_vma=False)
```

```python
import functools

import jax
import jax.numpy as jnp
from jax import lax
from jax.experimental import pallas as pl
from jax.experimental.pallas import tpu as pltpu
from jax.sharding import PartitionSpec as P

MESH = pl.DeviceIdType.MESH
NT = (((1,), (1,)), ((), ()))


def each(start, stop, body):
    if stop - start <= 4:
        for i in range(start, stop):
            body(i)
    else:
        lax.fori_loop(start, stop, lambda i, _: (body(i), None)[1], None)


def kernel(
    n_blk, n_dp, n_sub, images,
    feats_hbm, proj_hbm, cid_hbm, idx_hbm, assign_hbm,
    out_ref,
    feats_ref, proj_ref, cid_ref, idx_ref, assign_ref, plane, plane_key, far, far_key, part_out, part_in, ret_out, ret_in,
    load_sem, pe_send, pe_recv, pk_send, pk_recv, fe_send, fe_recv, fk_send, fk_recv,
    po_send, po_recv, re_send, re_recv,
):
    n_plane = n_dp * n_sub
    n_far = n_blk // 2
    whole_far = (n_blk - 1) // 2
    z, x, c = lax.axis_index("blk"), lax.axis_index("dp"), lax.axis_index("sub")
    rows = idx_ref.shape[1]

    def in_plane(k, sign):
        dx, dc = lax.div(k, n_sub), lax.rem(k, n_sub)
        if sign < 0:
            dx, dc = n_dp - dx, n_sub - dc
        return {"blk": z, "dp": lax.rem(x + dx, n_dp), "sub": lax.rem(c + dc, n_sub)}

    def across(d, sign):
        return {"blk": lax.rem(z + (d if sign > 0 else n_blk - d), n_blk), "dp": x, "sub": c}

    half = n_blk // 2
    lower = z < half
    within = jnp.where(lower, z, z - half)
    sends_half = (lax.rem(within, 2) == 0) == lower
    has_half = n_far > whole_far

    loads = [
        pltpu.make_async_copy(src, dst, load_sem.at[i])
        for i, (src, dst) in enumerate((
            (assign_hbm, assign_ref), (cid_hbm, cid_ref), (idx_hbm, idx_ref),
            (feats_hbm, feats_ref), (proj_hbm, proj_ref),
        ))
    ]
    for load in loads:
        load.start()

    barrier = pltpu.get_barrier_semaphore()

    def greet(device):
        pl.semaphore_signal(barrier, inc=1, device_id=device, device_id_type=MESH)

    each(1, n_plane, lambda k: greet(in_plane(k, 1)))

    def greet_far(d):
        greet(across(d, 1))
        greet(across(d, -1))

    each(1, whole_far + 1, greet_far)
    if has_half:
        greet(across(half, 1))
    pl.semaphore_wait(barrier, n_plane - 1 + 2 * whole_far + (1 if has_half else 0))

    def remote(src, dst, send, recv, device):
        return pltpu.make_async_remote_copy(
            src_ref=src, dst_ref=dst, send_sem=send, recv_sem=recv,
            device_id=device, device_id_type=MESH,
        )

    def plane_emb_copy(k):
        return remote(plane.at[0], plane.at[k], pe_send.at[k], pe_recv.at[k], in_plane(k, 1))

    def plane_key_copy(k):
        return remote(plane_key.at[0], plane_key.at[k], pk_send.at[k], pk_recv.at[k], in_plane(k, 1))

    def far_emb_copy(d):
        return remote(plane.at[0], far.at[d - 1], fe_send.at[d - 1], fe_recv.at[d - 1], across(d, 1))

    def far_key_copy(d):
        return remote(plane_key.at[0], far_key.at[d - 1], fk_send.at[d - 1], fk_recv.at[d - 1], across(d, 1))

    def part_copy(k):
        return remote(part_out.at[k], part_in.at[k], po_send.at[k], po_recv.at[k], in_plane(k, -1))

    def ret_copy(d):
        return remote(ret_out.at[d - 1], ret_in.at[d - 1], re_send.at[d - 1], re_recv.at[d - 1], across(d, -1))

    for load in loads[:3]:
        load.wait()
    per_coarse = assign_ref.shape[0] // n_dp
    cid = cid_ref[...]
    base = jnp.zeros_like(cid)
    for f in range(assign_ref.shape[0]):
        base = jnp.where(cid == f, lax.div(assign_ref[f], per_coarse) * images, base)
    key = base + idx_ref[...]
    sub_row = lax.broadcasted_iota(jnp.int32, (8, rows), 0)
    plane_key[0] = jnp.where(
        sub_row == 0, jnp.broadcast_to(key, (8, rows)), jnp.broadcast_to(base, (8, rows))
    )
    each(1, whole_far + 1, lambda d: far_key_copy(d).start())
    if has_half:
        pl.when(sends_half)(lambda: far_key_copy(half).start())
    each(1, n_plane, lambda k: plane_key_copy(k).start())

    loads[3].wait()
    feats = feats_ref[...].astype(jnp.float32)
    center = jnp.mean(feats, axis=1, keepdims=True)
    shifted = feats - center
    spread = jnp.mean(shifted * shifted, axis=1, keepdims=True)
    normed = (shifted * lax.rsqrt(spread + 1e-05)).astype(jnp.bfloat16)
    loads[4].wait()
    proj_out = jnp.dot(normed, proj_ref[...], preferred_element_type=jnp.float32)
    scale = lax.rsqrt(jnp.sum(proj_out * proj_out, axis=1, keepdims=True) + 1e-06)
    plane[0] = (proj_out * scale).astype(jnp.bfloat16)

    if has_half:
        pl.when(sends_half)(lambda: far_emb_copy(half).start())
    each(1, whole_far + 1, lambda d: far_emb_copy(d).start())
    each(1, n_plane, lambda k: plane_emb_copy(n_plane - k).start())

    def column(key_row):
        return jnp.transpose(jnp.broadcast_to(key_row, (rows, rows)))

    def lane_best(scores):
        return jnp.max(jnp.transpose(scores), axis=0, keepdims=True)

    def spread8(row):
        return jnp.broadcast_to(row, (8, rows))

    own_col = column(plane_key[0][0:1])

    def own_step(k, best):
        keys = plane_key[k]
        k_row, b_row = keys[0:1], keys[1:2]
        scores = lax.dot_general(plane[0], plane[k], NT, preferred_element_type=jnp.float32)
        good = (own_col >= b_row) & (own_col < b_row + images) & (own_col > k_row)
        return jnp.maximum(best, jnp.where(good, scores, -1.0))

    def arrived(k):
        plane_key_copy(k).wait_recv()
        plane_emb_copy(k).wait_recv()

    best = own_step(0, jnp.full((rows, rows), -1.0, jnp.float32))
    if n_plane <= 4:
        for k in range(1, n_plane):
            arrived(k)
            best = own_step(k, best)
    else:
        best = lax.fori_loop(1, n_plane, lambda k, b: (arrived(k), own_step(k, b))[1], best)
    total = lane_best(best)

    def far_step(d, first):
        far_key_copy(d).wait_recv()
        far_emb_copy(d).wait_recv()
        col = column(far_key[d - 1][0:1])

        def step(k, best):
            keys = plane_key[k]
            k_row, b_row = keys[0:1], keys[1:2]
            scores = lax.dot_general(far[d - 1], plane[k], NT, preferred_element_type=jnp.float32)
            scores = jnp.where((col >= b_row) & (col < b_row + images), scores, -1.0)
            low = col < k_row
            gain = spread8(jnp.max(jnp.where(low, scores, -1.0), axis=0, keepdims=True))
            if first:
                part_out[k] = gain
            else:
                part_out[k] = jnp.maximum(part_out[k], gain)
            return jnp.maximum(best, jnp.where(low, -1.0, scores))

        best = jnp.full((rows, rows), -1.0, jnp.float32)
        if n_plane <= 4:
            for k in range(n_plane):
                best = step(k, best)
        else:
            best = lax.fori_loop(0, n_plane, step, best)
        ret_out[d - 1] = spread8(lane_best(best))
        ret_copy(d).start()

    if whole_far == 0:
        part_out[...] = jnp.full(part_out.shape, -1.0, jnp.float32)
    else:
        far_step(1, True)
        each(2, whole_far + 1, lambda d: far_step(d, False))
    if has_half:
        pl.when(jnp.logical_not(sends_half))(lambda: far_step(half, False))
    each(1, n_plane, lambda k: part_copy(k).start())

    total = jnp.maximum(total, part_out[0][0:1])

    def take_part(k, total):
        part_copy(k).wait_recv()
        return jnp.maximum(total, part_in[k][0:1])

    def take_ret(d, total):
        ret_copy(d).wait_recv()
        return jnp.maximum(total, ret_in[d - 1][0:1])

    out_ref[...] = jnp.full(out_ref.shape, -1.0, jnp.float32)
    for d in range(1, whole_far + 1):
        total = take_ret(d, total)
    for k in range(1, n_plane):
        total = take_part(k, total)
    out_ref[...] = total
    if has_half:

        @pl.when(sends_half)
        def _():
            out_ref[...] = take_ret(half, out_ref[...])

    def sent_far(d):
        far_key_copy(d).wait_send()
        far_emb_copy(d).wait_send()

    def sent_plane(k):
        plane_key_copy(k).wait_send()
        plane_emb_copy(k).wait_send()
        part_copy(k).wait_send()

    each(1, whole_far + 1, sent_far)
    each(1, whole_far + 1, lambda d: ret_copy(d).wait_send())
    if has_half:
        pl.when(sends_half)(lambda: sent_far(half))
        pl.when(jnp.logical_not(sends_half))(lambda: ret_copy(half).wait_send())
    each(1, n_plane, sent_plane)


def local(n_blk, n_dp, n_sub, cls_feats, proj, cluster_id, row_index, assign):
    rows, depth = cls_feats.shape
    width = proj.shape[1]
    n_plane, n_far = n_dp * n_sub, max(1, n_blk // 2)
    images = rows * n_blk * n_plane
    vmem, dma = pltpu.VMEM, pltpu.SemaphoreType.DMA
    out = pl.pallas_call(
        functools.partial(kernel, n_blk, n_dp, n_sub, images),
        out_shape=jax.ShapeDtypeStruct((1, rows), jnp.float32),
        in_specs=[pl.BlockSpec(memory_space=pltpu.HBM)] * 5,
        out_specs=pl.BlockSpec(memory_space=vmem),
        scratch_shapes=[
            vmem((rows, depth), cls_feats.dtype),
            vmem((depth, width), proj.dtype),
            vmem((1, rows), jnp.int32),
            vmem((1, rows), jnp.int32),
            pltpu.SMEM(assign.shape, jnp.int32),
            vmem((n_plane, rows, width), jnp.bfloat16),
            vmem((n_plane, 8, rows), jnp.int32),
            vmem((n_far, rows, width), jnp.bfloat16),
            vmem((n_far, 8, rows), jnp.int32),
            vmem((n_plane, 8, rows), jnp.float32),
            vmem((n_plane, 8, rows), jnp.float32),
            vmem((n_far, 8, rows), jnp.float32),
            vmem((n_far, 8, rows), jnp.float32),
            dma((5,)),
            *[dma((n_plane,))] * 4,
            *[dma((n_far,))] * 4,
            *[dma((n_plane,))] * 2,
            *[dma((n_far,))] * 2,
        ],
        compiler_params=pltpu.CompilerParams(
            collective_id=0, has_side_effects=True, vmem_limit_bytes=56 * 2**20
        ),
    )(cls_feats, proj, cluster_id.reshape(1, rows), row_index.reshape(1, rows), assign)
    return out.reshape(rows)


def solution(mesh):
    split = ("groups", "blk", "dp", "sub")
    in_specs = (P(split, None), P(), P(split, None), P(split), P("groups"))
    body = functools.partial(local, mesh.shape["blk"], mesh.shape["dp"], mesh.shape["sub"])
    return jax.shard_map(body, mesh=mesh, in_specs=in_specs, out_specs=P(split), check_vma=False)
```

```python
import functools

import jax
import jax.numpy as jnp
from jax import lax
from jax.experimental import pallas as pl
from jax.experimental.pallas import tpu as pltpu
from jax.sharding import PartitionSpec as P

MESH = pl.DeviceIdType.MESH
NT = (((1,), (1,)), ((), ()))


def each(start, stop, body):
    if stop - start <= 4:
        for i in range(start, stop):
            body(i)
    else:
        lax.fori_loop(start, stop, lambda i, _: (body(i), None)[1], None)


def kernel(
    n_blk, n_dp, n_sub, images,
    feats_hbm, proj_hbm, cid_hbm, idx_hbm, assign_hbm,
    out_ref,
    feats_ref, proj_ref, cid_ref, idx_ref, assign_ref, plane, plane_key, far, far_key, part_out, part_in, ret_out, ret_in,
    load_sem, pe_send, pe_recv, pk_send, pk_recv, fe_send, fe_recv, fk_send, fk_recv,
    po_send, po_recv, re_send, re_recv,
):
    n_plane = n_dp * n_sub
    n_far = n_blk // 2
    whole_far = (n_blk - 1) // 2
    z, x, c = lax.axis_index("blk"), lax.axis_index("dp"), lax.axis_index("sub")
    rows = idx_ref.shape[1]

    def in_plane(k, sign):
        dx, dc = lax.div(k, n_sub), lax.rem(k, n_sub)
        if sign < 0:
            dx, dc = n_dp - dx, n_sub - dc
        return {"blk": z, "dp": lax.rem(x + dx, n_dp), "sub": lax.rem(c + dc, n_sub)}

    def across(d, sign):
        return {"blk": lax.rem(z + (d if sign > 0 else n_blk - d), n_blk), "dp": x, "sub": c}

    half = n_blk // 2
    lower = z < half
    within = jnp.where(lower, z, z - half)
    sends_half = (lax.rem(within, 2) == 0) == lower
    has_half = n_far > whole_far

    loads = [
        pltpu.make_async_copy(src, dst, load_sem.at[i])
        for i, (src, dst) in enumerate((
            (assign_hbm, assign_ref), (cid_hbm, cid_ref), (idx_hbm, idx_ref),
            (feats_hbm, feats_ref), (proj_hbm, proj_ref),
        ))
    ]
    for load in loads:
        load.start()

    barrier = pltpu.get_barrier_semaphore()

    def greet(device):
        pl.semaphore_signal(barrier, inc=1, device_id=device, device_id_type=MESH)

    each(1, n_plane, lambda k: greet(in_plane(k, 1)))

    def greet_far(d):
        greet(across(d, 1))
        greet(across(d, -1))

    each(1, whole_far + 1, greet_far)
    if has_half:
        greet(across(half, 1))
    pl.semaphore_wait(barrier, n_plane - 1 + 2 * whole_far + (1 if has_half else 0))

    def remote(src, dst, send, recv, device):
        return pltpu.make_async_remote_copy(
            src_ref=src, dst_ref=dst, send_sem=send, recv_sem=recv,
            device_id=device, device_id_type=MESH,
        )

    def plane_emb_copy(k):
        return remote(plane.at[0], plane.at[k], pe_send.at[k], pe_recv.at[k], in_plane(k, 1))

    def plane_key_copy(k):
        return remote(plane_key.at[0], plane_key.at[k], pk_send.at[k], pk_recv.at[k], in_plane(k, 1))

    def far_emb_copy(d):
        return remote(plane.at[0], far.at[d - 1], fe_send.at[d - 1], fe_recv.at[d - 1], across(d, 1))

    def far_key_copy(d):
        return remote(plane_key.at[0], far_key.at[d - 1], fk_send.at[d - 1], fk_recv.at[d - 1], across(d, 1))

    def part_copy(k):
        return remote(part_out.at[k], part_in.at[k], po_send.at[k], po_recv.at[k], in_plane(k, -1))

    def ret_copy(d):
        return remote(ret_out.at[d - 1], ret_in.at[d - 1], re_send.at[d - 1], re_recv.at[d - 1], across(d, -1))

    for load in loads[:3]:
        load.wait()
    per_coarse = assign_ref.shape[0] // n_dp
    cid = cid_ref[...]
    base = jnp.zeros_like(cid)
    for f in range(assign_ref.shape[0]):
        base = jnp.where(cid == f, lax.div(assign_ref[f], per_coarse) * images, base)
    key = base + idx_ref[...]
    sub_row = lax.broadcasted_iota(jnp.int32, (8, rows), 0)
    plane_key[0] = jnp.where(
        sub_row == 0, jnp.broadcast_to(key, (8, rows)), jnp.broadcast_to(base, (8, rows))
    )
    each(1, whole_far + 1, lambda d: far_key_copy(d).start())
    if has_half:
        pl.when(sends_half)(lambda: far_key_copy(half).start())
    each(1, n_plane, lambda k: plane_key_copy(k).start())

    loads[3].wait()
    feats = feats_ref[...].astype(jnp.float32)
    center = jnp.mean(feats, axis=1, keepdims=True)
    shifted = feats - center
    spread = jnp.mean(shifted * shifted, axis=1, keepdims=True)
    normed = (shifted * lax.rsqrt(spread + 1e-05)).astype(jnp.bfloat16)
    loads[4].wait()
    proj_out = jnp.dot(normed, proj_ref[...], preferred_element_type=jnp.float32)
    scale = lax.rsqrt(jnp.sum(proj_out * proj_out, axis=1, keepdims=True) + 1e-06)
    plane[0] = (proj_out * scale).astype(jnp.bfloat16)

    if has_half:
        pl.when(sends_half)(lambda: far_emb_copy(half).start())
    each(1, whole_far + 1, lambda d: far_emb_copy(d).start())
    each(1, n_plane, lambda k: plane_emb_copy(n_plane - k).start())

    def column(key_row):
        return jnp.transpose(jnp.broadcast_to(key_row, (rows, rows)))

    def lane_best(scores):
        return jnp.max(jnp.transpose(scores), axis=0, keepdims=True)

    def spread8(row):
        return jnp.broadcast_to(row, (8, rows))

    own_col = column(plane_key[0][0:1])

    def own_step(k, best):
        keys = plane_key[k]
        k_row, b_row = keys[0:1], keys[1:2]
        scores = lax.dot_general(plane[0], plane[k], NT, preferred_element_type=jnp.float32)
        good = (own_col >= b_row) & (own_col < b_row + images) & (own_col > k_row)
        return jnp.maximum(best, jnp.where(good, scores, -1.0))

    def arrived(k):
        plane_key_copy(k).wait_recv()
        plane_emb_copy(k).wait_recv()

    best = own_step(0, jnp.full((rows, rows), -1.0, jnp.float32))
    if n_plane <= 4:
        for k in range(1, n_plane):
            arrived(k)
            best = own_step(k, best)
    else:
        best = lax.fori_loop(1, n_plane, lambda k, b: (arrived(k), own_step(k, b))[1], best)
    total = lane_best(best)

    def far_step(d, first):
        far_key_copy(d).wait_recv()
        far_emb_copy(d).wait_recv()
        col = column(far_key[d - 1][0:1])

        def step(k, best):
            keys = plane_key[k]
            k_row, b_row = keys[0:1], keys[1:2]
            scores = lax.dot_general(far[d - 1], plane[k], NT, preferred_element_type=jnp.float32)
            scores = jnp.where((col >= b_row) & (col < b_row + images), scores, -1.0)
            low = col < k_row
            gain = spread8(jnp.max(jnp.where(low, scores, -1.0), axis=0, keepdims=True))
            if first:
                part_out[k] = gain
            else:
                part_out[k] = jnp.maximum(part_out[k], gain)
            return jnp.maximum(best, jnp.where(low, -1.0, scores))

        best = jnp.full((rows, rows), -1.0, jnp.float32)
        if n_plane <= 4:
            for k in range(n_plane):
                best = step(k, best)
        else:
            best = lax.fori_loop(0, n_plane, step, best)
        ret_out[d - 1] = spread8(lane_best(best))
        ret_copy(d).start()

    if whole_far == 0:
        part_out[...] = jnp.full(part_out.shape, -1.0, jnp.float32)
    else:
        far_step(1, True)
        each(2, whole_far + 1, lambda d: far_step(d, False))
    if has_half:
        pl.when(jnp.logical_not(sends_half))(lambda: far_step(half, False))
    each(1, n_plane, lambda k: part_copy(k).start())

    total = jnp.maximum(total, part_out[0][0:1])

    def take_part(k, total):
        part_copy(k).wait_recv()
        return jnp.maximum(total, part_in[k][0:1])

    def take_ret(d, total):
        ret_copy(d).wait_recv()
        return jnp.maximum(total, ret_in[d - 1][0:1])

    out_ref[...] = jnp.full(out_ref.shape, -1.0, jnp.float32)
    for d in range(1, whole_far + 1):
        total = take_ret(d, total)
    for k in range(1, n_plane):
        total = take_part(k, total)
    out_ref[...] = total
    if has_half:

        @pl.when(sends_half)
        def _():
            out_ref[...] = take_ret(half, out_ref[...])

    def sent_far(d):
        far_key_copy(d).wait_send()
        far_emb_copy(d).wait_send()

    def sent_plane(k):
        plane_key_copy(k).wait_send()
        plane_emb_copy(k).wait_send()
        part_copy(k).wait_send()

    each(1, whole_far + 1, sent_far)
    each(1, whole_far + 1, lambda d: ret_copy(d).wait_send())
    if has_half:
        pl.when(sends_half)(lambda: sent_far(half))
        pl.when(jnp.logical_not(sends_half))(lambda: ret_copy(half).wait_send())
    each(1, n_plane, sent_plane)


def local(n_blk, n_dp, n_sub, cls_feats, proj, cluster_id, row_index, assign):
    rows, depth = cls_feats.shape
    width = proj.shape[1]
    n_plane, n_far = n_dp * n_sub, max(1, n_blk // 2)
    images = rows * n_blk * n_plane
    vmem, dma = pltpu.VMEM, pltpu.SemaphoreType.DMA
    out = pl.pallas_call(
        functools.partial(kernel, n_blk, n_dp, n_sub, images),
        out_shape=pltpu.VMEM((1, rows), jnp.float32),
        in_specs=[pl.BlockSpec(memory_space=pltpu.HBM)] * 5,
        out_specs=pl.BlockSpec(memory_space=vmem),
        scratch_shapes=[
            vmem((rows, depth), cls_feats.dtype),
            vmem((depth, width), proj.dtype),
            vmem((1, rows), jnp.int32),
            vmem((1, rows), jnp.int32),
            pltpu.SMEM(assign.shape, jnp.int32),
            vmem((n_plane, rows, width), jnp.bfloat16),
            vmem((n_plane, 8, rows), jnp.int32),
            vmem((n_far, rows, width), jnp.bfloat16),
            vmem((n_far, 8, rows), jnp.int32),
            vmem((n_plane, 8, rows), jnp.float32),
            vmem((n_plane, 8, rows), jnp.float32),
            vmem((n_far, 8, rows), jnp.float32),
            vmem((n_far, 8, rows), jnp.float32),
            dma((5,)),
            *[dma((n_plane,))] * 4,
            *[dma((n_far,))] * 4,
            *[dma((n_plane,))] * 2,
            *[dma((n_far,))] * 2,
        ],
        compiler_params=pltpu.CompilerParams(
            collective_id=0, has_side_effects=True, vmem_limit_bytes=56 * 2**20
        ),
    )(cls_feats, proj, cluster_id.reshape(1, rows), row_index.reshape(1, rows), assign)
    return out.reshape(rows)


def solution(mesh):
    split = ("groups", "blk", "dp", "sub")
    in_specs = (P(split, None), P(), P(split, None), P(split), P("groups"))
    body = functools.partial(local, mesh.shape["blk"], mesh.shape["dp"], mesh.shape["sub"])
    return jax.shard_map(body, mesh=mesh, in_specs=in_specs, out_specs=P(split), check_vma=False)
```

```python
import functools

import jax
import jax.numpy as jnp
from jax import lax
from jax.experimental import pallas as pl
from jax.experimental.pallas import tpu as pltpu
from jax.sharding import PartitionSpec as P

MESH = pl.DeviceIdType.MESH
NT = (((1,), (1,)), ((), ()))


def each(start, stop, body):
    if stop - start <= 4:
        for i in range(start, stop):
            body(i)
    else:
        lax.fori_loop(start, stop, lambda i, _: (body(i), None)[1], None)


def kernel(
    n_blk, n_dp, n_sub, images,
    feats_hbm, proj_hbm, cid_hbm, idx_hbm, assign_hbm,
    out_ref,
    feats_ref, proj_ref, cid_ref, idx_ref, assign_ref, plane, plane_key, far, far_key, part_out, part_in, ret_out, ret_in,
    load_sem, pe_send, pe_recv, pk_send, pk_recv, fe_send, fe_recv, fk_send, fk_recv,
    po_send, po_recv, re_send, re_recv,
):
    n_plane = n_dp * n_sub
    n_far = n_blk // 2
    whole_far = (n_blk - 1) // 2
    z, x, c = lax.axis_index("blk"), lax.axis_index("dp"), lax.axis_index("sub")
    rows = idx_ref.shape[1]

    def in_plane(k, sign):
        dx, dc = lax.div(k, n_sub), lax.rem(k, n_sub)
        if sign < 0:
            dx, dc = n_dp - dx, n_sub - dc
        return {"blk": z, "dp": lax.rem(x + dx, n_dp), "sub": lax.rem(c + dc, n_sub)}

    def across(d, sign):
        return {"blk": lax.rem(z + (d if sign > 0 else n_blk - d), n_blk), "dp": x, "sub": c}

    half = n_blk // 2
    lower = z < half
    within = jnp.where(lower, z, z - half)
    sends_half = (lax.rem(within, 2) == 0) == lower
    has_half = n_far > whole_far

    loads = [
        pltpu.make_async_copy(src, dst, load_sem.at[i])
        for i, (src, dst) in enumerate((
            (assign_hbm, assign_ref), (cid_hbm, cid_ref), (idx_hbm, idx_ref),
            (feats_hbm, feats_ref), (proj_hbm, proj_ref),
        ))
    ]
    for load in loads:
        load.start()

    barrier = pltpu.get_barrier_semaphore()

    def greet(device):
        pl.semaphore_signal(barrier, inc=1, device_id=device, device_id_type=MESH)

    each(1, n_plane, lambda k: greet(in_plane(k, 1)))

    def greet_far(d):
        greet(across(d, 1))
        greet(across(d, -1))

    each(1, whole_far + 1, greet_far)
    if has_half:
        greet(across(half, 1))
    pl.semaphore_wait(barrier, n_plane - 1 + 2 * whole_far + (1 if has_half else 0))

    def remote(src, dst, send, recv, device):
        return pltpu.make_async_remote_copy(
            src_ref=src, dst_ref=dst, send_sem=send, recv_sem=recv,
            device_id=device, device_id_type=MESH,
        )

    def plane_emb_copy(k):
        return remote(plane.at[0], plane.at[k], pe_send.at[k], pe_recv.at[k], in_plane(k, 1))

    def plane_key_copy(k):
        return remote(plane_key.at[0], plane_key.at[k], pk_send.at[k], pk_recv.at[k], in_plane(k, 1))

    piece = rows // 2

    def far_emb_copy(d, h):
        part = pl.ds(h * piece, piece)
        return remote(
            plane.at[0, part], far.at[d - 1, part],
            fe_send.at[d - 1, h], fe_recv.at[d - 1, h], across(d, 1),
        )

    def far_key_copy(d):
        return remote(plane_key.at[0], far_key.at[d - 1], fk_send.at[d - 1], fk_recv.at[d - 1], across(d, 1))

    def part_copy(k):
        return remote(part_out.at[k], part_in.at[k], po_send.at[k], po_recv.at[k], in_plane(k, -1))

    def ret_copy(d):
        return remote(ret_out.at[d - 1], ret_in.at[d - 1], re_send.at[d - 1], re_recv.at[d - 1], across(d, -1))

    for load in loads[:3]:
        load.wait()
    per_coarse = assign_ref.shape[0] // n_dp
    cid = cid_ref[...]
    base = jnp.zeros_like(cid)
    for f in range(assign_ref.shape[0]):
        base = jnp.where(cid == f, lax.div(assign_ref[f], per_coarse) * images, base)
    key = base + idx_ref[...]
    sub_row = lax.broadcasted_iota(jnp.int32, (8, rows), 0)
    plane_key[0] = jnp.where(
        sub_row == 0, jnp.broadcast_to(key, (8, rows)), jnp.broadcast_to(base, (8, rows))
    )
    each(1, whole_far + 1, lambda d: far_key_copy(d).start())
    if has_half:
        pl.when(sends_half)(lambda: far_key_copy(half).start())
    each(1, n_plane, lambda k: plane_key_copy(k).start())

    loads[3].wait()
    feats = feats_ref[...].astype(jnp.float32)
    center = jnp.mean(feats, axis=1, keepdims=True)
    shifted = feats - center
    spread = jnp.mean(shifted * shifted, axis=1, keepdims=True)
    normed = (shifted * lax.rsqrt(spread + 1e-05)).astype(jnp.bfloat16)
    loads[4].wait()
    proj_out = jnp.dot(normed, proj_ref[...], preferred_element_type=jnp.float32)
    scale = lax.rsqrt(jnp.sum(proj_out * proj_out, axis=1, keepdims=True) + 1e-06)
    plane[0] = (proj_out * scale).astype(jnp.bfloat16)

    if has_half:
        pl.when(sends_half)(lambda: far_emb_copy(half, 0).start())
    each(1, whole_far + 1, lambda d: far_emb_copy(d, 0).start())
    if has_half:
        pl.when(sends_half)(lambda: far_emb_copy(half, 1).start())
    each(1, whole_far + 1, lambda d: far_emb_copy(d, 1).start())
    each(1, n_plane, lambda k: plane_emb_copy(n_plane - k).start())

    def column(key_row):
        return jnp.transpose(jnp.broadcast_to(key_row, (rows, rows)))

    def lane_best(scores):
        return jnp.max(jnp.transpose(scores), axis=0, keepdims=True)

    def spread8(row):
        return jnp.broadcast_to(row, (8, rows))

    own_col = column(plane_key[0][0:1])

    def own_step(k, best):
        keys = plane_key[k]
        k_row, b_row = keys[0:1], keys[1:2]
        scores = lax.dot_general(plane[0], plane[k], NT, preferred_element_type=jnp.float32)
        good = (own_col >= b_row) & (own_col < b_row + images) & (own_col > k_row)
        return jnp.maximum(best, jnp.where(good, scores, -1.0))

    def arrived(k):
        plane_key_copy(k).wait_recv()
        plane_emb_copy(k).wait_recv()

    best = own_step(0, jnp.full((rows, rows), -1.0, jnp.float32))
    if n_plane <= 4:
        for k in range(1, n_plane):
            arrived(k)
            best = own_step(k, best)
    else:
        best = lax.fori_loop(1, n_plane, lambda k, b: (arrived(k), own_step(k, b))[1], best)
    total = lane_best(best)

    def far_step(d, first):
        far_key_copy(d).wait_recv()
        whole_col = column(far_key[d - 1][0:1])
        halves = []
        for h in range(2):
            far_emb_copy(d, h).wait_recv()
            span = slice(h * piece, (h + 1) * piece)
            col = whole_col[span]
            fresh = first and h == 0

            def step(k, best):
                keys = plane_key[k]
                k_row, b_row = keys[0:1], keys[1:2]
                scores = lax.dot_general(far[d - 1, span], plane[k], NT, preferred_element_type=jnp.float32)
                scores = jnp.where((col >= b_row) & (col < b_row + images), scores, -1.0)
                low = col < k_row
                gain = spread8(jnp.max(jnp.where(low, scores, -1.0), axis=0, keepdims=True))
                part_out[k] = gain if fresh else jnp.maximum(part_out[k], gain)
                return jnp.maximum(best, jnp.where(low, -1.0, scores))

            best = jnp.full((piece, rows), -1.0, jnp.float32)
            if n_plane <= 4:
                for k in range(n_plane):
                    best = step(k, best)
            else:
                best = lax.fori_loop(0, n_plane, step, best)
            halves.append(best)
        best = jnp.concatenate(halves, axis=0)
        ret_out[d - 1] = spread8(lane_best(best))
        ret_copy(d).start()

    if whole_far == 0:
        part_out[...] = jnp.full(part_out.shape, -1.0, jnp.float32)
    else:
        far_step(1, True)
        each(2, whole_far + 1, lambda d: far_step(d, False))
    if has_half:
        pl.when(jnp.logical_not(sends_half))(lambda: far_step(half, False))
    each(1, n_plane, lambda k: part_copy(k).start())

    total = jnp.maximum(total, part_out[0][0:1])

    def take_part(k, total):
        part_copy(k).wait_recv()
        return jnp.maximum(total, part_in[k][0:1])

    def take_ret(d, total):
        ret_copy(d).wait_recv()
        return jnp.maximum(total, ret_in[d - 1][0:1])

    out_ref[...] = jnp.full(out_ref.shape, -1.0, jnp.float32)
    for d in range(1, whole_far + 1):
        total = take_ret(d, total)
    for k in range(1, n_plane):
        total = take_part(k, total)
    out_ref[...] = total
    if has_half:

        @pl.when(sends_half)
        def _():
            out_ref[...] = take_ret(half, out_ref[...])

    def sent_far(d):
        far_key_copy(d).wait_send()
        far_emb_copy(d, 0).wait_send()
        far_emb_copy(d, 1).wait_send()

    def sent_plane(k):
        plane_key_copy(k).wait_send()
        plane_emb_copy(k).wait_send()
        part_copy(k).wait_send()

    each(1, whole_far + 1, sent_far)
    each(1, whole_far + 1, lambda d: ret_copy(d).wait_send())
    if has_half:
        pl.when(sends_half)(lambda: sent_far(half))
        pl.when(jnp.logical_not(sends_half))(lambda: ret_copy(half).wait_send())
    each(1, n_plane, sent_plane)


def local(n_blk, n_dp, n_sub, cls_feats, proj, cluster_id, row_index, assign):
    rows, depth = cls_feats.shape
    width = proj.shape[1]
    n_plane, n_far = n_dp * n_sub, max(1, n_blk // 2)
    images = rows * n_blk * n_plane
    vmem, dma = pltpu.VMEM, pltpu.SemaphoreType.DMA
    out = pl.pallas_call(
        functools.partial(kernel, n_blk, n_dp, n_sub, images),
        out_shape=pltpu.VMEM((1, rows), jnp.float32),
        in_specs=[pl.BlockSpec(memory_space=pltpu.HBM)] * 5,
        out_specs=pl.BlockSpec(memory_space=vmem),
        scratch_shapes=[
            vmem((rows, depth), cls_feats.dtype),
            vmem((depth, width), proj.dtype),
            vmem((1, rows), jnp.int32),
            vmem((1, rows), jnp.int32),
            pltpu.SMEM(assign.shape, jnp.int32),
            vmem((n_plane, rows, width), jnp.bfloat16),
            vmem((n_plane, 8, rows), jnp.int32),
            vmem((n_far, rows, width), jnp.bfloat16),
            vmem((n_far, 8, rows), jnp.int32),
            vmem((n_plane, 8, rows), jnp.float32),
            vmem((n_plane, 8, rows), jnp.float32),
            vmem((n_far, 8, rows), jnp.float32),
            vmem((n_far, 8, rows), jnp.float32),
            dma((5,)),
            *[dma((n_plane,))] * 4,
            *[dma((n_far, 2))] * 2,
            *[dma((n_far,))] * 2,
            *[dma((n_plane,))] * 2,
            *[dma((n_far,))] * 2,
        ],
        compiler_params=pltpu.CompilerParams(
            collective_id=0, has_side_effects=True, vmem_limit_bytes=56 * 2**20
        ),
    )(cls_feats, proj, cluster_id.reshape(1, rows), row_index.reshape(1, rows), assign)
    return out.reshape(rows)


def solution(mesh):
    split = ("groups", "blk", "dp", "sub")
    in_specs = (P(split, None), P(), P(split, None), P(split), P("groups"))
    body = functools.partial(local, mesh.shape["blk"], mesh.shape["dp"], mesh.shape["sub"])
    return jax.shard_map(body, mesh=mesh, in_specs=in_specs, out_specs=P(split), check_vma=False)
```
